32 devices in a mesh: row: 8 (over z, x), col: 4 (over y, core).
Axes of the slice: x: 2, y: 2, z: 4, core: 2. Of those that a mesh axis runs over, the one named last changes fastest.
Arguments:
- activations: bfloat16 [1024, 5120], P('row'), may hold values from -6 to 6
- act_basis: bfloat16 [5120, 5120], P('row', 'col'), may hold values from -0.078125 to 0.078125
- gradients: bfloat16 [1024, 27648], P('row', 'col'), may hold values from -6 to 6
- grad_basis: bfloat16 [27648, 27648], P('col', 'row'), may hold values from -0.0390625 to 0.0390625
Outputs:
- correction: float32 [5120, 27648], P('col', 'row')
The draws below stay inside these ranges and needn't reach their ends.
All inputs are finite; a program needn't handle non-finite values.
Results may differ from the reference program's by a relative error of at most 0.0041.
Values may be sent and summed in bfloat16 or wider, within the bound.
A program may use at most 192 MiB of HBM per device.

```python
import jax
import jax.numpy as jnp
from jax import lax

D = 5120
FF = 27648
SEQ_LEN = 512
SEQS = 2
TOKENS = 1024


def block_scale(stream_key, dims, pieces, smallest, largest):
    level, own = 1.0, jax.random.fold_in(stream_key, 6)
    for dim, shards_of in pieces:
        draws = jnp.exp(jax.random.uniform(jax.random.fold_in(own, dim), (shards_of,), jnp.float32, smallest / len(pieces), largest / len(pieces)))
        level = level * jnp.repeat(draws, dims[dim] // shards_of).reshape([-1 if axis == dim else 1 for axis in range(len(dims))])
    return level


def scatter_about(stream_key, shape, spread, limit, split=(), dtype=jnp.bfloat16):
    array = spread * jax.random.normal(stream_key, shape, jnp.float32)
    if split:
        array = array * block_scale(stream_key, shape, split, -0.22, 0.18)
    return jnp.clip(array, -limit, limit).astype(dtype)


def setup_inputs(seed: int = 0) -> dict:
    splits = jax.random.split(jax.random.key(seed), 5)
    activations = scatter_about(splits[0], (TOKENS, D), 1.0, 6.0, ((0, 8),))
    act_basis = scatter_about(splits[1], (D, D), D ** -0.5, 0.078125, ((0, 8), (1, 4)))
    gradients = scatter_about(splits[2], (TOKENS, FF), 1.0, 6.0, ((0, 8), (1, 4)))
    grad_basis = scatter_about(splits[3], (FF, FF), FF ** -0.5, 0.0390625, ((0, 4), (1, 8)))
    return {"activations": activations, "act_basis": act_basis, "gradients": gradients, "grad_basis": grad_basis}


def reference(activations, act_basis, gradients, grad_basis):
    rotated_acts = jnp.dot(activations, act_basis, preferred_element_type=jnp.float32).astype(jnp.bfloat16)
    rotated_grads = jnp.dot(gradients, grad_basis, preferred_element_type=jnp.float32).astype(jnp.bfloat16)
    total = jnp.zeros((D, FF), jnp.float32)
    for seq_index in range(SEQS):
        acts_seq = rotated_acts[seq_index * SEQ_LEN:(seq_index + 1) * SEQ_LEN]
        grads_seq = rotated_grads[seq_index * SEQ_LEN:(seq_index + 1) * SEQ_LEN]
        seq_grad = lax.dot_general(acts_seq, grads_seq, (((0,), (0,)), ((), ())), preferred_element_type=jnp.float32)
        total = total + seq_grad * seq_grad
    return total / (SEQS * SEQ_LEN)
```

```python
import functools

import jax
import jax.numpy as jnp
from jax import lax
from jax.experimental import pallas as pl
from jax.experimental.pallas import tpu as pltpu
from jax.sharding import PartitionSpec as P

SEQ_LEN = 512
SEQS = 2
MESH = pl.DeviceIdType.MESH
MIB = 1 << 20


def row_of(position, n):
    x = position // (n // 2)
    z = position + x * (n - 1 - 2 * position)
    return 2 * z + x


def column_tiles(columns):
    wide = 768
    starts = [(i * wide, wide) for i in range(columns // wide)]
    rest = columns % wide
    if rest:
        starts.append((columns - rest, rest))
    return starts


def grads_kernel(n, m, g_ref, w_ref, out_ref, gath_ref, xv, wv, part, total, ysend, fin, core_in, y_in,
                 ring_send, ring_recv, load_sem, w_sem, core_send, core_recv, y_send, y_recv,
                 fin_send, fin_recv, fin_local):
    rows, depth = g_ref.shape
    half, quarter = rows // 2, rows // 4
    row = lax.axis_index("row")
    col = lax.axis_index("col")
    x = row % 2
    z = row // 2
    pos = z + x * (n - 1 - 2 * z)
    core = col % 2
    chip = col // 2
    right = row_of((pos + 1) % n, n)
    left = row_of((pos + n - 1) % n, n)
    ring = ((right, col), (left, col))
    pair = (row, chip * 2 + 1 - core)
    others = [(row, ((chip + k) % m) * 2 + core) for k in range(1, m)]

    barrier = pltpu.get_barrier_semaphore()
    for peer in (*ring, pair, *others):
        pl.semaphore_signal(barrier, inc=1, device_id=peer, device_id_type=MESH)
    pl.semaphore_wait(barrier, 3 + len(others))

    def piece(d, u):
        return pl.ds((d * 2 + u) * quarter, quarter)

    def ring_copy(src, step, d, u):
        return pltpu.make_async_remote_copy(
            src_ref=src, dst_ref=gath_ref.at[step + 1, piece(d, u)],
            send_sem=ring_send.at[step, d, u], recv_sem=ring_recv.at[step + 1, d, u],
            device_id=ring[d], device_id_type=MESH)

    for u in range(2):
        for d in range(2):
            ring_copy(g_ref.at[piece(d, u)], 0, d, u).start()
    pltpu.make_async_copy(g_ref, xv.at[0], load_sem.at[0]).start()
    chunk = depth // 4
    loads = [pltpu.make_async_copy(w_ref.at[pl.ds(i * chunk, chunk)], wv.at[pl.ds(i * chunk, chunk)], w_sem.at[i])
             for i in range(4)]
    for load in loads:
        load.start()

    def arrive(step, u):
        for d in range(2):
            ring_copy(gath_ref.at[step - 1, piece(d, u)], step - 1, d, u).wait_recv()

            @pl.when(step < n - 1)
            def _():
                ring_copy(gath_ref.at[step, piece(d, u)], step, d, u).start()

    def core_copy(step):
        return pltpu.make_async_remote_copy(
            src_ref=part.at[1 - core], dst_ref=core_in.at[step % 2],
            send_sem=core_send, recv_sem=core_recv.at[step % 2], device_id=pair, device_id_type=MESH)

    def y_copy(step, k):
        return pltpu.make_async_remote_copy(
            src_ref=ysend, dst_ref=y_in.at[step % 2, k],
            send_sem=y_send.at[k], recv_sem=y_recv.at[step % 2, k], device_id=others[k], device_id_type=MESH)

    def out_row(step):
        return row_of((pos + n + (2 * core - 1) * step) % n, n)

    def fin_copy(step):
        place = out_ref.at[out_row(step), core]
        return pltpu.make_async_remote_copy(
            src_ref=fin, dst_ref=place,
            send_sem=fin_send, recv_sem=fin_recv.at[step], device_id=pair, device_id_type=MESH)

    def fin_store(step):
        return pltpu.make_async_copy(fin, out_ref.at[out_row(step), core], fin_local)

    def over_chips(step):
        core_copy(step).wait_recv()

        @pl.when(step > 0)
        def _():
            for k in range(m - 1):
                y_copy(step - 1, k).wait_send()

        total[...] = part[core] + core_in[step % 2]
        ysend[...] = total[...].astype(ysend.dtype)
        for k in range(m - 1):
            y_copy(step, k).start()

    def finish(step):
        for k in range(m - 1):
            y_copy(step, k).wait_recv()

        @pl.when(step > 0)
        def _():
            fin_copy(step - 1).wait_send()
            fin_store(step - 1).wait()

        value = total[...]
        for k in range(m - 1):
            value += y_in[step % 2, k].astype(jnp.float32)
        fin[...] = value.astype(fin.dtype)
        fin_copy(step).start()
        fin_store(step).start()

    columns = w_ref.shape[1]
    tiles = column_tiles(columns)
    wide = tiles[0][1]
    whole = columns // wide
    early = whole // 2

    def multiply(slot, start, width):
        product = jnp.dot(xv[slot], wv[:, pl.ds(start, width)], preferred_element_type=jnp.float32)
        part[0, :, pl.ds(start, width)] = product[:half]
        part[1, :, pl.ds(start, width)] = product[half:]

    def step_body(step, carry):
        slot = step % 2

        @pl.when(step < n - 1)
        def _():
            arrive(step + 1, 0)

        @pl.when(step > 1)
        def _():
            finish(step - 2)

        @pl.when(step > 0)
        def _():
            over_chips(step - 1)
            core_copy(step - 1).wait_send()

        pltpu.make_async_copy(g_ref, xv.at[slot], load_sem.at[slot]).wait()

        @pl.when(step == 0)
        def _():
            for load in loads:
                load.wait()

        @pl.loop(0, early)
        def _(j):
            multiply(slot, pl.multiple_of(j * wide, wide), wide)

        @pl.when(step < n - 1)
        def _():
            arrive(step + 1, 1)
            pltpu.make_async_copy(gath_ref.at[step + 1], xv.at[1 - slot], load_sem.at[1 - slot]).start()

        @pl.loop(early, whole)
        def _(j):
            multiply(slot, pl.multiple_of(j * wide, wide), wide)

        for start, width in tiles[whole:]:
            multiply(slot, start, width)
        core_copy(step).start()
        return carry

    lax.fori_loop(0, n, step_body, 0)
    finish(n - 2)
    over_chips(n - 1)
    core_copy(n - 1).wait_send()
    finish(n - 1)
    for k in range(m - 1):
        y_copy(n - 1, k).wait_send()
    fin_copy(n - 1).wait_send()
    fin_store(n - 1).wait()
    for step in range(n):
        pltpu.make_async_remote_copy(
            src_ref=fin, dst_ref=out_ref.at[row, 1 - core], send_sem=fin_send, recv_sem=fin_recv.at[step],
            device_id=pair, device_id_type=MESH).wait_recv()
    for step in range(n - 1):
        for u in range(2):
            for d in range(2):
                ring_copy(g_ref.at[piece(d, u)], step, d, u).wait_send()


def rotate_grads(gradients, grad_basis, n, m):
    rows, depth = gradients.shape
    columns = grad_basis.shape[1]
    half = rows // 2
    f32, bf16 = jnp.float32, jnp.bfloat16
    dma = pltpu.SemaphoreType.DMA
    rotated, _ = pl.pallas_call(
        functools.partial(grads_kernel, n, m),
        out_shape=[jax.ShapeDtypeStruct((n, 2, half, columns), bf16),
                   jax.ShapeDtypeStruct((n, rows, depth), bf16)],
        in_specs=[pl.BlockSpec(memory_space=pl.ANY)] * 2,
        out_specs=[pl.BlockSpec(memory_space=pl.ANY)] * 2,
        scratch_shapes=[
            pltpu.VMEM((2, rows, depth), bf16),
            pltpu.VMEM((depth, columns), bf16),
            pltpu.VMEM((2, half, columns), f32),
            pltpu.VMEM((half, columns), f32),
            pltpu.VMEM((half, columns), bf16),
            pltpu.VMEM((half, columns), bf16),
            pltpu.VMEM((2, half, columns), f32),
            pltpu.VMEM((2, m - 1, half, columns), bf16),
            dma((n, 2, 2)), dma((n, 2, 2)), dma((2,)), dma((4,)),
            dma, dma((2,)), dma((m - 1,)), dma((2, m - 1)),
            dma, dma((n,)), dma,
        ],
        compiler_params=pltpu.CompilerParams(
            collective_id=0, has_side_effects=True, vmem_limit_bytes=60 * MIB),
        cost_estimate=pl.CostEstimate(
            flops=2 * n * rows * depth * columns, bytes_accessed=2 * depth * columns, transcendentals=0),
    )(gradients, grad_basis)
    return rotated.reshape(n * rows, columns)


def correct_kernel(acts_ref, grads_ref, out_ref, turned):
    @pl.when(pl.program_id(0) == 0)
    def _():
        for i in range(turned.shape[0]):
            turned[i] = acts_ref[:, i * turned.shape[1]:(i + 1) * turned.shape[1]].T

    acts = turned[pl.program_id(0)]
    for start, width in column_tiles(grads_ref.shape[1]):
        place = pl.ds(start, width)
        value = None
        for seq in range(SEQS):
            tokens = slice(seq * SEQ_LEN, (seq + 1) * SEQ_LEN)
            grad = jnp.dot(acts[:, tokens], grads_ref[tokens, place], preferred_element_type=jnp.float32)
            value = grad * grad if value is None else value + grad * grad
        out_ref[:, place] = value * (1.0 / (SEQS * SEQ_LEN))


def correct(rotated_acts, rotated_grads):
    tokens, width = rotated_acts.shape
    columns = rotated_grads.shape[1]
    block = 256
    return pl.pallas_call(
        correct_kernel,
        out_shape=jax.ShapeDtypeStruct((width, columns), jnp.float32),
        grid=(width // block,),
        in_specs=[pl.BlockSpec((tokens, width), lambda i: (0, 0)), pl.BlockSpec((tokens, columns), lambda i: (0, 0))],
        out_specs=pl.BlockSpec((block, columns), lambda i: (i, 0)),
        scratch_shapes=[pltpu.VMEM((width // block, block, tokens), jnp.bfloat16)],
        compiler_params=pltpu.CompilerParams(vmem_limit_bytes=56 * MIB),
        cost_estimate=pl.CostEstimate(
            flops=2 * tokens * width * columns, bytes_accessed=4 * width * columns, transcendentals=0),
    )(rotated_acts, rotated_grads)


def rotate_acts(activations, act_basis):
    mine = lax.all_to_all(activations, "row", split_axis=1, concat_axis=0, tiled=True)
    part = jnp.dot(mine, act_basis, preferred_element_type=jnp.float32)
    own = lax.psum_scatter(part, "row", scatter_dimension=0, tiled=True).astype(jnp.bfloat16)
    return lax.all_gather(own, "row", axis=0, tiled=True)


def local_plain(activations, act_basis, gradients, grad_basis):
    rotated_acts = rotate_acts(activations, act_basis)
    partial_grads = jnp.dot(
        lax.all_gather(gradients, "row", axis=0, tiled=True), grad_basis, preferred_element_type=jnp.float32)
    rotated_grads = lax.psum(partial_grads, "col").astype(jnp.bfloat16)
    total = 0.0
    for seq in range(SEQS):
        tokens = slice(seq * SEQ_LEN, (seq + 1) * SEQ_LEN)
        grad = lax.dot_general(rotated_acts[tokens], rotated_grads[tokens], (((0,), (0,)), ((), ())),
                               preferred_element_type=jnp.float32)
        total = total + grad * grad
    return total / (SEQS * SEQ_LEN)


def local_kernels(n, m, activations, act_basis, gradients, grad_basis):
    rotated_grads = rotate_grads(gradients, grad_basis, n, m)
    rotated_acts = rotate_acts(activations, act_basis)
    return correct(rotated_acts, rotated_grads)


def solution(mesh):
    n, columns = mesh.shape["row"], mesh.shape["col"]

    def local(activations, act_basis, gradients, grad_basis):
        rows, depth = gradients.shape
        held = 2 * depth * grad_basis.shape[1]
        tiled = rows % 64 == 0 and depth % 128 == 0 and grad_basis.shape[1] % 128 == 0 and act_basis.shape[1] % 256 == 0
        if n % 2 == 0 and n > 2 and columns % 2 == 0 and columns > 2 and tiled and held < 46 * MIB:
            return local_kernels(n, columns // 2, activations, act_basis, gradients, grad_basis)
        return local_plain(activations, act_basis, gradients, grad_basis)

    return jax.shard_map(
        local,
        mesh=mesh,
        in_specs=(P("row", None), P("row", "col"), P("row", "col"), P("col", "row")),
        out_specs=P("col", "row"),
        check_vma=False,
    )
```

```python
import functools

import jax
import jax.numpy as jnp
from jax import lax
from jax.experimental import pallas as pl
from jax.experimental.pallas import tpu as pltpu
from jax.sharding import PartitionSpec as P

SEQ_LEN = 512
SEQS = 2
MESH = pl.DeviceIdType.MESH
MIB = 1 << 20


def row_of(position, n):
    x = position // (n // 2)
    z = position + x * (n - 1 - 2 * position)
    return 2 * z + x


def column_tiles(columns):
    wide = 768
    starts = [(i * wide, wide) for i in range(columns // wide)]
    rest = columns % wide
    if rest:
        starts.append((columns - rest, rest))
    return starts


def rotate_kernel(n, m, g_ref, w_ref, a_ref, b_ref, out_ref, acts_ref, gath_ref,
                  xv, wv, part, total, ysend, fin, core_in, y_in, mine, basis, sums_in, sums_out, own,
                  ring_send, ring_recv, load_sem, w_sem, core_send, core_recv, y_send, y_recv,
                  fin_send, fin_recv, fin_local, mine_send, mine_recv, basis_sem,
                  sums_send, sums_recv, own_local, acts_send, acts_recv):
    rows, depth = g_ref.shape
    half, quarter = rows // 2, rows // 4
    row = lax.axis_index("row")
    col = lax.axis_index("col")
    x = row % 2
    z = row // 2
    pos = z + x * (n - 1 - 2 * z)
    core = col % 2
    chip = col // 2
    right = row_of((pos + 1) % n, n)
    left = row_of((pos + n - 1) % n, n)
    ring = ((right, col), (left, col))
    pair = (row, chip * 2 + 1 - core)
    others = [(row, ((chip + k) % m) * 2 + core) for k in range(1, m)]

    barrier = pltpu.get_barrier_semaphore()
    rows_peers = [((row + k) % n, col) for k in range(1, n)]
    for peer in (*rows_peers, pair, *others):
        pl.semaphore_signal(barrier, inc=1, device_id=peer, device_id_type=MESH)
    pl.semaphore_wait(barrier, n + len(others))

    def piece(d, u):
        return pl.ds((d * 2 + u) * quarter, quarter)

    def ring_copy(src, step, d, u):
        return pltpu.make_async_remote_copy(
            src_ref=src, dst_ref=gath_ref.at[step + 1, piece(d, u)],
            send_sem=ring_send.at[step, d, u], recv_sem=ring_recv.at[step + 1, d, u],
            device_id=ring[d], device_id_type=MESH)

    inner = b_ref.shape[0]

    def inputs_of(target):
        return a_ref.at[:, pl.ds(pl.multiple_of(target * inner, 128), inner)]

    def mine_copy(k):
        target, _ = rows_peers[k - 1]
        return pltpu.make_async_remote_copy(
            src_ref=inputs_of(target), dst_ref=mine.at[row],
            send_sem=mine_send.at[k], recv_sem=mine_recv.at[k], device_id=(target, col), device_id_type=MESH)

    for d in range(2):
        ring_copy(g_ref.at[piece(d, 0)], 0, d, 0).start()
    for k in range(1, n):
        mine_copy(k).start()
    mine_own = pltpu.make_async_copy(inputs_of(row), mine.at[row], mine_send.at[0])
    mine_own.start()
    basis_load = pltpu.make_async_copy(b_ref, basis, basis_sem)
    basis_load.start()
    for d in range(2):
        ring_copy(g_ref.at[piece(d, 1)], 0, d, 1).start()
    pltpu.make_async_copy(g_ref, xv.at[0], load_sem.at[0]).start()
    chunk = depth // 4
    loads = [pltpu.make_async_copy(w_ref.at[pl.ds(i * chunk, chunk)], wv.at[pl.ds(i * chunk, chunk)], w_sem.at[i])
             for i in range(4)]
    for load in loads:
        load.start()

    def arrive(step, u):
        for d in range(2):
            ring_copy(gath_ref.at[step - 1, piece(d, u)], step - 1, d, u).wait_recv()

            @pl.when(step < n - 1)
            def _():
                ring_copy(gath_ref.at[step, piece(d, u)], step, d, u).start()

    def sums_copy(turn, d):
        return pltpu.make_async_remote_copy(
            src_ref=sums_out.at[turn % 2, d], dst_ref=sums_in.at[turn % 4, d],
            send_sem=sums_send.at[turn, d], recv_sem=sums_recv.at[turn, d], device_id=ring[d], device_id_type=MESH)

    def holder(steps, d):
        return row_of((pos + 2 * n - (1 - 2 * d) * steps) % n, n)

    def acts_copy(src, turn, d):
        return pltpu.make_async_remote_copy(
            src_ref=src, dst_ref=acts_ref.at[holder(turn, d), d],
            send_sem=acts_send.at[turn, d], recv_sem=acts_recv.at[turn, d], device_id=ring[d], device_id_type=MESH)

    def own_copy(d):
        return pltpu.make_async_copy(own.at[d], acts_ref.at[row, d], own_local.at[d])

    def acts_turn(turn):
        @pl.when(turn == 0)
        def _():
            for k in range(1, n):
                mine_copy(k).wait_recv()
            mine_own.wait()
            basis_load.wait()

        @pl.when(turn < n)
        def _():
            for d in range(2):
                product = jnp.dot(mine[holder(turn + 1, d), d * half:(d + 1) * half], basis[...],
                                  preferred_element_type=jnp.float32)

                @pl.when(turn == 0)
                def _():
                    sums_out[0, d] = product
                    sums_copy(turn, d).start()

                @pl.when(turn > 0)
                def _():
                    sums_copy(turn - 1, d).wait_recv()

                @pl.when((turn > 0) & (turn < n - 1))
                def _():
                    @pl.when(turn > 1)
                    def _():
                        sums_copy(turn - 2, d).wait_send()

                    sums_out[turn % 2, d] = product + sums_in[(turn + 3) % 4, d]
                    sums_copy(turn, d).start()

                @pl.when(turn == n - 1)
                def _():
                    own[d] = (product + sums_in[(turn + 3) % 4, d]).astype(own.dtype)
                    own_copy(d).start()
                    acts_copy(own.at[d], 0, d).start()

        @pl.when(turn >= n)
        def _():
            for d in range(2):
                hop = turn - (n - 1)
                acts_copy(own.at[d], hop - 1, d).wait_recv()
                acts_copy(acts_ref.at[holder(hop, d), d], hop, d).start()

    def core_copy(step):
        return pltpu.make_async_remote_copy(
            src_ref=part.at[1 - core], dst_ref=core_in.at[step % 2],
            send_sem=core_send, recv_sem=core_recv.at[step % 2], device_id=pair, device_id_type=MESH)

    def y_copy(step, k):
        return pltpu.make_async_remote_copy(
            src_ref=ysend, dst_ref=y_in.at[step % 2, k],
            send_sem=y_send.at[k], recv_sem=y_recv.at[step % 2, k], device_id=others[k], device_id_type=MESH)

    def out_row(step):
        return row_of((pos + n + (2 * core - 1) * step) % n, n)

    def fin_copy(step):
        place = out_ref.at[out_row(step), core]
        return pltpu.make_async_remote_copy(
            src_ref=fin, dst_ref=place,
            send_sem=fin_send, recv_sem=fin_recv.at[step], device_id=pair, device_id_type=MESH)

    def fin_store(step):
        return pltpu.make_async_copy(fin, out_ref.at[out_row(step), core], fin_local)

    def over_chips(step):
        core_copy(step).wait_recv()

        @pl.when(step > 0)
        def _():
            for k in range(m - 1):
                y_copy(step - 1, k).wait_send()

        total[...] = part[core] + core_in[step % 2]
        ysend[...] = total[...].astype(ysend.dtype)
        for k in range(m - 1):
            y_copy(step, k).start()

    def finish(step):
        for k in range(m - 1):
            y_copy(step, k).wait_recv()

        @pl.when(step > 0)
        def _():
            fin_copy(step - 1).wait_send()
            fin_store(step - 1).wait()

        value = total[...]
        for k in range(m - 1):
            value += y_in[step % 2, k].astype(jnp.float32)
        fin[...] = value.astype(fin.dtype)
        fin_copy(step).start()
        fin_store(step).start()

    columns = w_ref.shape[1]
    tiles = column_tiles(columns)
    wide = tiles[0][1]
    whole = columns // wide
    early = whole // 2

    def multiply(slot, start, width):
        product = jnp.dot(xv[slot], wv[:, pl.ds(start, width)], preferred_element_type=jnp.float32)
        part[0, :, pl.ds(start, width)] = product[:half]
        part[1, :, pl.ds(start, width)] = product[half:]

    def step_body(step, carry):
        slot = step % 2

        @pl.when(step < n - 1)
        def _():
            arrive(step + 1, 0)
            acts_turn(2 * step)

        @pl.when(step > 1)
        def _():
            finish(step - 2)

        @pl.when(step > 0)
        def _():
            over_chips(step - 1)
            core_copy(step - 1).wait_send()

        pltpu.make_async_copy(g_ref, xv.at[slot], load_sem.at[slot]).wait()

        @pl.when(step == 0)
        def _():
            for load in loads:
                load.wait()

        @pl.loop(0, early)
        def _(j):
            multiply(slot, pl.multiple_of(j * wide, wide), wide)

        @pl.when(step < n - 1)
        def _():
            arrive(step + 1, 1)
            pltpu.make_async_copy(gath_ref.at[step + 1], xv.at[1 - slot], load_sem.at[1 - slot]).start()
            acts_turn(2 * step + 1)

        @pl.loop(early, whole)
        def _(j):
            multiply(slot, pl.multiple_of(j * wide, wide), wide)

        for start, width in tiles[whole:]:
            multiply(slot, start, width)
        core_copy(step).start()
        return carry

    lax.fori_loop(0, n, step_body, 0)
    finish(n - 2)
    over_chips(n - 1)
    core_copy(n - 1).wait_send()
    finish(n - 1)
    for k in range(m - 1):
        y_copy(n - 1, k).wait_send()
    fin_copy(n - 1).wait_send()
    fin_store(n - 1).wait()
    for step in range(n):
        pltpu.make_async_remote_copy(
            src_ref=fin, dst_ref=out_ref.at[row, 1 - core], send_sem=fin_send, recv_sem=fin_recv.at[step],
            device_id=pair, device_id_type=MESH).wait_recv()
    for step in range(n - 1):
        for u in range(2):
            for d in range(2):
                ring_copy(g_ref.at[piece(d, u)], step, d, u).wait_send()
    for d in range(2):
        acts_copy(own.at[d], n - 2, d).wait_recv()
        own_copy(d).wait()
        for turn in range(n - 3, n - 1):
            sums_copy(turn, d).wait_send()
        for turn in range(n - 1):
            acts_copy(own.at[d], turn, d).wait_send()
    for k in range(1, n):
        mine_copy(k).wait_send()


def rotate(activations, act_basis, gradients, grad_basis, n, m):
    rows, depth = gradients.shape
    inner, width = act_basis.shape
    columns = grad_basis.shape[1]
    half = rows // 2
    f32, bf16 = jnp.float32, jnp.bfloat16
    dma = pltpu.SemaphoreType.DMA
    grads, acts, _ = pl.pallas_call(
        functools.partial(rotate_kernel, n, m),
        out_shape=[jax.ShapeDtypeStruct((n, 2, half, columns), bf16),
                   jax.ShapeDtypeStruct((n, 2, half, width), bf16),
                   jax.ShapeDtypeStruct((n, rows, depth), bf16)],
        in_specs=[pl.BlockSpec(memory_space=pl.ANY)] * 4,
        out_specs=[pl.BlockSpec(memory_space=pl.ANY)] * 3,
        scratch_shapes=[
            pltpu.VMEM((2, rows, depth), bf16),
            pltpu.VMEM((depth, columns), bf16),
            pltpu.VMEM((2, half, columns), f32),
            pltpu.VMEM((half, columns), f32),
            pltpu.VMEM((half, columns), bf16),
            pltpu.VMEM((half, columns), bf16),
            pltpu.VMEM((2, half, columns), f32),
            pltpu.VMEM((2, m - 1, half, columns), bf16),
            pltpu.VMEM((n, rows, inner), bf16),
            pltpu.VMEM((inner, width), bf16),
            pltpu.VMEM((4, 2, half, width), f32),
            pltpu.VMEM((2, 2, half, width), f32),
            pltpu.VMEM((2, half, width), bf16),
            dma((n, 2, 2)), dma((n, 2, 2)), dma((2,)), dma((4,)),
            dma, dma((2,)), dma((m - 1,)), dma((2, m - 1)),
            dma, dma((n,)), dma, dma((n,)), dma((n,)), dma,
            dma((n, 2)), dma((n, 2)), dma((2,)), dma((n, 2)), dma((n, 2)),
        ],
        compiler_params=pltpu.CompilerParams(
            collective_id=0, has_side_effects=True, vmem_limit_bytes=63 * MIB),
        cost_estimate=pl.CostEstimate(
            flops=2 * n * rows * depth * columns, bytes_accessed=2 * depth * columns, transcendentals=0),
    )(gradients, grad_basis, activations, act_basis)
    return acts.reshape(n * rows, width), grads.reshape(n * rows, columns)


def correct_kernel(acts_ref, grads_ref, out_ref, turned):
    @pl.when(pl.program_id(0) == 0)
    def _():
        for i in range(turned.shape[0]):
            turned[i] = acts_ref[:, i * turned.shape[1]:(i + 1) * turned.shape[1]].T

    acts = turned[pl.program_id(0)]
    for start, width in column_tiles(grads_ref.shape[1]):
        place = pl.ds(start, width)
        value = None
        for seq in range(SEQS):
            tokens = slice(seq * SEQ_LEN, (seq + 1) * SEQ_LEN)
            grad = jnp.dot(acts[:, tokens], grads_ref[tokens, place], preferred_element_type=jnp.float32)
            value = grad * grad if value is None else value + grad * grad
        out_ref[:, place] = value * (1.0 / (SEQS * SEQ_LEN))


def correct(rotated_acts, rotated_grads):
    tokens, width = rotated_acts.shape
    columns = rotated_grads.shape[1]
    block = 256
    return pl.pallas_call(
        correct_kernel,
        out_shape=jax.ShapeDtypeStruct((width, columns), jnp.float32),
        grid=(width // block,),
        in_specs=[pl.BlockSpec((tokens, width), lambda i: (0, 0)), pl.BlockSpec((tokens, columns), lambda i: (0, 0))],
        out_specs=pl.BlockSpec((block, columns), lambda i: (i, 0)),
        scratch_shapes=[pltpu.VMEM((width // block, block, tokens), jnp.bfloat16)],
        compiler_params=pltpu.CompilerParams(vmem_limit_bytes=56 * MIB),
        cost_estimate=pl.CostEstimate(
            flops=2 * tokens * width * columns, bytes_accessed=4 * width * columns, transcendentals=0),
    )(rotated_acts, rotated_grads)


def rotate_acts(activations, act_basis):
    mine = lax.all_to_all(activations, "row", split_axis=1, concat_axis=0, tiled=True)
    part = jnp.dot(mine, act_basis, preferred_element_type=jnp.float32)
    own = lax.psum_scatter(part, "row", scatter_dimension=0, tiled=True).astype(jnp.bfloat16)
    return lax.all_gather(own, "row", axis=0, tiled=True)


def local_plain(activations, act_basis, gradients, grad_basis):
    rotated_acts = rotate_acts(activations, act_basis)
    partial_grads = jnp.dot(
        lax.all_gather(gradients, "row", axis=0, tiled=True), grad_basis, preferred_element_type=jnp.float32)
    rotated_grads = lax.psum(partial_grads, "col").astype(jnp.bfloat16)
    total = 0.0
    for seq in range(SEQS):
        tokens = slice(seq * SEQ_LEN, (seq + 1) * SEQ_LEN)
        grad = lax.dot_general(rotated_acts[tokens], rotated_grads[tokens], (((0,), (0,)), ((), ())),
                               preferred_element_type=jnp.float32)
        total = total + grad * grad
    return total / (SEQS * SEQ_LEN)


def local_kernels(n, m, activations, act_basis, gradients, grad_basis):
    rotated_acts, rotated_grads = rotate(activations, act_basis, gradients, grad_basis, n, m)
    return correct(rotated_acts, rotated_grads)


def solution(mesh):
    n, columns = mesh.shape["row"], mesh.shape["col"]

    def local(activations, act_basis, gradients, grad_basis):
        rows, depth = gradients.shape
        held = 2 * depth * grad_basis.shape[1]
        tiled = rows % 64 == 0 and depth % 128 == 0 and grad_basis.shape[1] % 128 == 0 and act_basis.shape[1] % 256 == 0 and act_basis.shape[0] % 128 == 0
        if n % 2 == 0 and n > 2 and columns % 2 == 0 and columns > 2 and tiled and held < 46 * MIB:
            return local_kernels(n, columns // 2, activations, act_basis, gradients, grad_basis)
        return local_plain(activations, act_basis, gradients, grad_basis)

    return jax.shard_map(
        local,
        mesh=mesh,
        in_specs=(P("row", None), P("row", "col"), P("row", "col"), P("col", "row")),
        out_specs=P("col", "row"),
        check_vma=False,
    )
```

```python
import functools

import jax
import jax.numpy as jnp
from jax import lax
from jax.experimental import pallas as pl
from jax.experimental.pallas import tpu as pltpu
from jax.sharding import PartitionSpec as P

SEQ_LEN = 512
SEQS = 2
MESH = pl.DeviceIdType.MESH
MIB = 1 << 20


def row_of(position, n):
    x = position // (n // 2)
    z = position + x * (n - 1 - 2 * position)
    return 2 * z + x


def column_tiles(columns):
    wide = 768
    starts = [(i * wide, wide) for i in range(columns // wide)]
    rest = columns % wide
    if rest:
        starts.append((columns - rest, rest))
    return starts


def rotate_kernel(n, m, g_ref, w_ref, a_ref, b_ref, out_ref, acts_ref, gath_ref,
                  xv, wv, part, total, ysend, fin, core_in, y_in, mine, basis, sums_in, sums_out, own,
                  ring_send, ring_recv, load_sem, w_sem, core_send, core_recv, y_send, y_recv,
                  fin_send, fin_recv, fin_local, mine_send, mine_recv, basis_sem,
                  sums_send, sums_recv, own_local, acts_send, acts_recv, swap_send, swap_recv):
    rows, depth = g_ref.shape
    half, quarter = rows // 2, rows // 4
    row = lax.axis_index("row")
    col = lax.axis_index("col")
    x = row % 2
    z = row // 2
    pos = z + x * (n - 1 - 2 * z)
    core = col % 2
    chip = col // 2
    right = row_of((pos + 1) % n, n)
    left = row_of((pos + n - 1) % n, n)
    ring = ((right, col), (left, col))
    pair = (row, chip * 2 + 1 - core)
    others = [(row, ((chip + k) % m) * 2 + core) for k in range(1, m)]

    barrier = pltpu.get_barrier_semaphore()
    rows_peers = [((row + k) % n, col) for k in range(1, n)]
    for peer in (*rows_peers, pair, *others):
        pl.semaphore_signal(barrier, inc=1, device_id=peer, device_id_type=MESH)
    pl.semaphore_wait(barrier, n + len(others))

    def piece(d, u):
        return pl.ds((d * 2 + u) * quarter, quarter)

    def ring_copy(src, step, d, u):
        return pltpu.make_async_remote_copy(
            src_ref=src, dst_ref=gath_ref.at[step + 1, piece(d, u)],
            send_sem=ring_send.at[step, d, u], recv_sem=ring_recv.at[step + 1, d, u],
            device_id=ring[d], device_id_type=MESH)

    inner = b_ref.shape[0]

    def inputs_of(target):
        return a_ref.at[:, pl.ds(pl.multiple_of(target * inner, 128), inner)]

    share = pl.ds(pl.multiple_of(core * half, half), half)

    def mine_copy(k):
        target, _ = rows_peers[k - 1]
        return pltpu.make_async_remote_copy(
            src_ref=a_ref.at[share, pl.ds(pl.multiple_of(target * inner, 128), inner)], dst_ref=mine.at[row, share],
            send_sem=mine_send.at[k], recv_sem=mine_recv.at[k], device_id=(target, col), device_id_type=MESH)

    def swap_copy(k):
        held = mine.at[(row + n - k) % n, share]
        return pltpu.make_async_remote_copy(
            src_ref=held, dst_ref=held, send_sem=swap_send.at[k], recv_sem=swap_recv.at[k],
            device_id=pair, device_id_type=MESH)

    for d in range(2):
        ring_copy(g_ref.at[piece(d, 0)], 0, d, 0).start()
    for k in range(1, n):
        mine_copy(k).start()
    mine_own = pltpu.make_async_copy(inputs_of(row), mine.at[row], mine_send.at[0])
    mine_own.start()
    basis_load = pltpu.make_async_copy(b_ref, basis, basis_sem)
    basis_load.start()
    for d in range(2):
        ring_copy(g_ref.at[piece(d, 1)], 0, d, 1).start()
    pltpu.make_async_copy(g_ref, xv.at[0], load_sem.at[0]).start()
    chunk = depth // 4
    loads = [pltpu.make_async_copy(w_ref.at[pl.ds(i * chunk, chunk)], wv.at[pl.ds(i * chunk, chunk)], w_sem.at[i])
             for i in range(4)]
    for load in loads:
        load.start()

    def arrive(step, u):
        for d in range(2):
            ring_copy(gath_ref.at[step - 1, piece(d, u)], step - 1, d, u).wait_recv()

            @pl.when(step < n - 1)
            def _():
                ring_copy(gath_ref.at[step, piece(d, u)], step, d, u).start()

    def sums_copy(turn, d):
        return pltpu.make_async_remote_copy(
            src_ref=sums_out.at[turn % 2, d], dst_ref=sums_in.at[turn % 4, d],
            send_sem=sums_send.at[turn, d], recv_sem=sums_recv.at[turn, d], device_id=ring[d], device_id_type=MESH)

    def holder(steps, d):
        return row_of((pos + 2 * n - (1 - 2 * d) * steps) % n, n)

    def acts_copy(src, turn, d):
        return pltpu.make_async_remote_copy(
            src_ref=src, dst_ref=acts_ref.at[holder(turn, d), d],
            send_sem=acts_send.at[turn, d], recv_sem=acts_recv.at[turn, d], device_id=ring[d], device_id_type=MESH)

    def own_copy(d):
        return pltpu.make_async_copy(own.at[d], acts_ref.at[row, d], own_local.at[d])

    def acts_turn(turn):
        @pl.when(turn == 0)
        def _():
            for k in range(1, n):
                mine_copy(k).wait_recv()
                swap_copy(k).start()
            for k in range(1, n):
                swap_copy(k).wait_recv()
            mine_own.wait()
            basis_load.wait()

        @pl.when(turn < n)
        def _():
            for d in range(2):
                product = jnp.dot(mine[holder(turn + 1, d), d * half:(d + 1) * half], basis[...],
                                  preferred_element_type=jnp.float32)

                @pl.when(turn == 0)
                def _():
                    sums_out[0, d] = product
                    sums_copy(turn, d).start()

                @pl.when(turn > 0)
                def _():
                    sums_copy(turn - 1, d).wait_recv()

                @pl.when((turn > 0) & (turn < n - 1))
                def _():
                    @pl.when(turn > 1)
                    def _():
                        sums_copy(turn - 2, d).wait_send()

                    sums_out[turn % 2, d] = product + sums_in[(turn + 3) % 4, d]
                    sums_copy(turn, d).start()

                @pl.when(turn == n - 1)
                def _():
                    own[d] = (product + sums_in[(turn + 3) % 4, d]).astype(own.dtype)
                    own_copy(d).start()
                    acts_copy(own.at[d], 0, d).start()

        @pl.when(turn >= n)
        def _():
            for d in range(2):
                hop = turn - (n - 1)
                acts_copy(own.at[d], hop - 1, d).wait_recv()
                acts_copy(acts_ref.at[holder(hop, d), d], hop, d).start()

    columns = w_ref.shape[1]
    tiles = column_tiles(columns)
    wide = tiles[0][1]
    whole = columns // wide
    early = whole // 2
    cuts = (pl.ds(0, early * wide), pl.ds(early * wide, columns - early * wide))

    def core_copy(step, cut):
        return pltpu.make_async_remote_copy(
            src_ref=part.at[1 - core, :, cuts[cut]], dst_ref=core_in.at[step % 2, :, cuts[cut]],
            send_sem=core_send.at[cut], recv_sem=core_recv.at[step % 2, cut], device_id=pair, device_id_type=MESH)

    def y_copy(step, k, cut):
        return pltpu.make_async_remote_copy(
            src_ref=ysend.at[:, cuts[cut]], dst_ref=y_in.at[step % 2, k, :, cuts[cut]],
            send_sem=y_send.at[k, cut], recv_sem=y_recv.at[step % 2, k, cut],
            device_id=others[k], device_id_type=MESH)

    def out_row(step):
        return row_of((pos + n + (2 * core - 1) * step) % n, n)

    def fin_copy(step, cut):
        return pltpu.make_async_remote_copy(
            src_ref=fin.at[:, cuts[cut]], dst_ref=out_ref.at[out_row(step), core, :, cuts[cut]],
            send_sem=fin_send.at[cut], recv_sem=fin_recv.at[step, cut], device_id=pair, device_id_type=MESH)

    def fin_store(step, cut):
        return pltpu.make_async_copy(
            fin.at[:, cuts[cut]], out_ref.at[out_row(step), core, :, cuts[cut]], fin_local.at[cut])

    def over_chips(step):
        for cut, place in enumerate(cuts):
            core_copy(step, cut).wait_recv()

            @pl.when(step > 0)
            def _():
                for k in range(m - 1):
                    y_copy(step - 1, k, cut).wait_send()

            value = part[core, :, place] + core_in[step % 2, :, place]
            total[:, place] = value
            ysend[:, place] = value.astype(ysend.dtype)
            for k in range(m - 1):
                y_copy(step, k, cut).start()

    def finish(step):
        for cut, place in enumerate(cuts):
            for k in range(m - 1):
                y_copy(step, k, cut).wait_recv()

            @pl.when(step > 0)
            def _():
                fin_copy(step - 1, cut).wait_send()
                fin_store(step - 1, cut).wait()

            value = total[:, place]
            for k in range(m - 1):
                value += y_in[step % 2, k, :, place].astype(jnp.float32)
            fin[:, place] = value.astype(fin.dtype)
            fin_copy(step, cut).start()
            fin_store(step, cut).start()

    def core_sent(step):
        for cut in range(2):
            core_copy(step, cut).wait_send()

    def multiply(slot, start, width):
        product = jnp.dot(xv[slot], wv[:, pl.ds(start, width)], preferred_element_type=jnp.float32)
        part[0, :, pl.ds(start, width)] = product[:half]
        part[1, :, pl.ds(start, width)] = product[half:]

    def step_body(step, carry):
        slot = step % 2

        @pl.when(step < n - 1)
        def _():
            arrive(step + 1, 0)
            acts_turn(2 * step)

        @pl.when(step > 1)
        def _():
            finish(step - 2)

        @pl.when(step > 0)
        def _():
            over_chips(step - 1)
            core_sent(step - 1)

        pltpu.make_async_copy(g_ref, xv.at[slot], load_sem.at[slot]).wait()

        @pl.when(step == 0)
        def _():
            for load in loads:
                load.wait()

        @pl.loop(0, early)
        def _(j):
            multiply(slot, pl.multiple_of(j * wide, wide), wide)

        core_copy(step, 0).start()

        @pl.when(step < n - 1)
        def _():
            arrive(step + 1, 1)
            pltpu.make_async_copy(gath_ref.at[step + 1], xv.at[1 - slot], load_sem.at[1 - slot]).start()
            acts_turn(2 * step + 1)

        @pl.loop(early, whole)
        def _(j):
            multiply(slot, pl.multiple_of(j * wide, wide), wide)

        for start, width in tiles[whole:]:
            multiply(slot, start, width)
        core_copy(step, 1).start()
        return carry

    lax.fori_loop(0, n, step_body, 0)
    finish(n - 2)
    over_chips(n - 1)
    core_sent(n - 1)
    finish(n - 1)
    for cut in range(2):
        for k in range(m - 1):
            y_copy(n - 1, k, cut).wait_send()
        fin_copy(n - 1, cut).wait_send()
        fin_store(n - 1, cut).wait()
        for step in range(n):
            pltpu.make_async_remote_copy(
                src_ref=fin.at[:, cuts[cut]], dst_ref=out_ref.at[row, 1 - core, :, cuts[cut]],
                send_sem=fin_send.at[cut], recv_sem=fin_recv.at[step, cut],
                device_id=pair, device_id_type=MESH).wait_recv()
    for step in range(n - 1):
        for u in range(2):
            for d in range(2):
                ring_copy(g_ref.at[piece(d, u)], step, d, u).wait_send()
    for d in range(2):
        acts_copy(own.at[d], n - 2, d).wait_recv()
        own_copy(d).wait()
        for turn in range(n - 3, n - 1):
            sums_copy(turn, d).wait_send()
        for turn in range(n - 1):
            acts_copy(own.at[d], turn, d).wait_send()
    for k in range(1, n):
        mine_copy(k).wait_send()
        swap_copy(k).wait_send()


def rotate(activations, act_basis, gradients, grad_basis, n, m):
    rows, depth = gradients.shape
    inner, width = act_basis.shape
    columns = grad_basis.shape[1]
    half = rows // 2
    f32, bf16 = jnp.float32, jnp.bfloat16
    dma = pltpu.SemaphoreType.DMA
    grads, acts, _ = pl.pallas_call(
        functools.partial(rotate_kernel, n, m),
        out_shape=[jax.ShapeDtypeStruct((n, 2, half, columns), bf16),
                   jax.ShapeDtypeStruct((n, 2, half, width), bf16),
                   jax.ShapeDtypeStruct((n, rows, depth), bf16)],
        in_specs=[pl.BlockSpec(memory_space=pl.ANY)] * 4,
        out_specs=[pl.BlockSpec(memory_space=pl.ANY)] * 3,
        scratch_shapes=[
            pltpu.VMEM((2, rows, depth), bf16),
            pltpu.VMEM((depth, columns), bf16),
            pltpu.VMEM((2, half, columns), f32),
            pltpu.VMEM((half, columns), f32),
            pltpu.VMEM((half, columns), bf16),
            pltpu.VMEM((half, columns), bf16),
            pltpu.VMEM((2, half, columns), f32),
            pltpu.VMEM((2, m - 1, half, columns), bf16),
            pltpu.VMEM((n, rows, inner), bf16),
            pltpu.VMEM((inner, width), bf16),
            pltpu.VMEM((4, 2, half, width), f32),
            pltpu.VMEM((2, 2, half, width), f32),
            pltpu.VMEM((2, half, width), bf16),
            dma((n, 2, 2)), dma((n, 2, 2)), dma((2,)), dma((4,)),
            dma((2,)), dma((2, 2)), dma((m - 1, 2)), dma((2, m - 1, 2)),
            dma((2,)), dma((n, 2)), dma((2,)), dma((n,)), dma((n,)), dma,
            dma((n, 2)), dma((n, 2)), dma((2,)), dma((n, 2)), dma((n, 2)), dma((n,)), dma((n,)),
        ],
        compiler_params=pltpu.CompilerParams(
            collective_id=0, has_side_effects=True, vmem_limit_bytes=63 * MIB),
        cost_estimate=pl.CostEstimate(
            flops=2 * n * rows * depth * columns, bytes_accessed=2 * depth * columns, transcendentals=0),
    )(gradients, grad_basis, activations, act_basis)
    return acts.reshape(n * rows, width), grads.reshape(n * rows, columns)


def correct_kernel(acts_ref, grads_ref, out_ref, turned):
    @pl.when(pl.program_id(0) == 0)
    def _():
        for i in range(turned.shape[0]):
            turned[i] = acts_ref[:, i * turned.shape[1]:(i + 1) * turned.shape[1]].T

    acts = turned[pl.program_id(0)]
    for start, width in column_tiles(grads_ref.shape[1]):
        place = pl.ds(start, width)
        value = None
        for seq in range(SEQS):
            tokens = slice(seq * SEQ_LEN, (seq + 1) * SEQ_LEN)
            grad = jnp.dot(acts[:, tokens], grads_ref[tokens, place], preferred_element_type=jnp.float32)
            value = grad * grad if value is None else value + grad * grad
        out_ref[:, place] = value * (1.0 / (SEQS * SEQ_LEN))


def correct(rotated_acts, rotated_grads):
    tokens, width = rotated_acts.shape
    columns = rotated_grads.shape[1]
    block = 256
    return pl.pallas_call(
        correct_kernel,
        out_shape=jax.ShapeDtypeStruct((width, columns), jnp.float32),
        grid=(width // block,),
        in_specs=[pl.BlockSpec((tokens, width), lambda i: (0, 0)), pl.BlockSpec((tokens, columns), lambda i: (0, 0))],
        out_specs=pl.BlockSpec((block, columns), lambda i: (i, 0)),
        scratch_shapes=[pltpu.VMEM((width // block, block, tokens), jnp.bfloat16)],
        compiler_params=pltpu.CompilerParams(vmem_limit_bytes=56 * MIB),
        cost_estimate=pl.CostEstimate(
            flops=2 * tokens * width * columns, bytes_accessed=4 * width * columns, transcendentals=0),
    )(rotated_acts, rotated_grads)


def rotate_acts(activations, act_basis):
    mine = lax.all_to_all(activations, "row", split_axis=1, concat_axis=0, tiled=True)
    part = jnp.dot(mine, act_basis, preferred_element_type=jnp.float32)
    own = lax.psum_scatter(part, "row", scatter_dimension=0, tiled=True).astype(jnp.bfloat16)
    return lax.all_gather(own, "row", axis=0, tiled=True)


def local_plain(activations, act_basis, gradients, grad_basis):
    rotated_acts = rotate_acts(activations, act_basis)
    partial_grads = jnp.dot(
        lax.all_gather(gradients, "row", axis=0, tiled=True), grad_basis, preferred_element_type=jnp.float32)
    rotated_grads = lax.psum(partial_grads, "col").astype(jnp.bfloat16)
    total = 0.0
    for seq in range(SEQS):
        tokens = slice(seq * SEQ_LEN, (seq + 1) * SEQ_LEN)
        grad = lax.dot_general(rotated_acts[tokens], rotated_grads[tokens], (((0,), (0,)), ((), ())),
                               preferred_element_type=jnp.float32)
        total = total + grad * grad
    return total / (SEQS * SEQ_LEN)


def local_kernels(n, m, activations, act_basis, gradients, grad_basis):
    rotated_acts, rotated_grads = rotate(activations, act_basis, gradients, grad_basis, n, m)
    return correct(rotated_acts, rotated_grads)


def solution(mesh):
    n, columns = mesh.shape["row"], mesh.shape["col"]

    def local(activations, act_basis, gradients, grad_basis):
        rows, depth = gradients.shape
        held = 2 * depth * grad_basis.shape[1]
        tiled = rows % 64 == 0 and depth % 128 == 0 and grad_basis.shape[1] % 128 == 0 and act_basis.shape[1] % 256 == 0 and act_basis.shape[0] % 128 == 0
        if n % 2 == 0 and n > 2 and columns % 2 == 0 and columns > 2 and tiled and held < 46 * MIB:
            return local_kernels(n, columns // 2, activations, act_basis, gradients, grad_basis)
        return local_plain(activations, act_basis, gradients, grad_basis)

    return jax.shard_map(
        local,
        mesh=mesh,
        in_specs=(P("row", None), P("row", "col"), P("row", "col"), P("col", "row")),
        out_specs=P("col", "row"),
        check_vma=False,
    )
```
